32 devices in a mesh: row: 8 (over y, x, core), pair: 4 (over z).
Axes of the slice: x: 2, y: 2, z: 4, core: 2. Of those that a mesh axis runs over, the one named last changes fastest.
Arguments:
- matrix: float32 [16384, 512], P('row', 'pair'), may hold values from -80 to 80
- partner: int32 [3, 4], replicated, may hold values from 0 to 3, as said below
Outputs:
- result: float32 [16384, 512], P('row', 'pair')
The draws below stay inside these ranges and needn't reach their ends.
Inputs may be any that keep to these rules, and one draw needn't show every extreme that they name: partner[r, j] equals j XOR s_r, where s_r is a power of two below 4 and the same for every j of round r.
All inputs are finite; a program needn't handle non-finite values.
Results may differ from the reference program's by a relative error of at most 0.0003.
Values sent between devices are 32-bit elements; how exact they have to be, the bound alone decides.
No kernel may reach another device: no remote copies, remote signals or barrier semaphores. Data moves between devices by JAX's collectives and lax.ppermute only.
A program may use at most 64 MiB of HBM per device.

```python
import math
import jax
import jax.numpy as jnp
from jax import lax

B = 64
ROUNDS = 4
NS_ITERS = 6
ROWS = 16384
COLS = 512
N_PAIR = 4


def draw_matrix(key, part):
    key_row, key_col, key_base = jax.random.split(key, 3)
    ramp = 1.0 + 2.0 * jnp.arange(ROWS, dtype=jnp.float32) / (ROWS - 1)
    rough_row = jnp.exp(jax.random.uniform(key_row, (ROWS,), jnp.float32, 0.0, math.log(4.0)))
    column_scale = jnp.exp(jax.random.uniform(key_col, (COLS,), jnp.float32, 0.0, math.log(10.0)))
    base = jnp.clip(jax.random.normal(key_base, (ROWS, COLS), jnp.float32), -6.0, 6.0)
    return (0.1 * base * (ramp * rough_row)[:, None] * column_scale[None, :]).astype(jnp.float32)


def draw_partner(key, part):
    bit_total = N_PAIR.bit_length() - 1
    bits = jax.random.randint(key, (ROUNDS - 1,), 0, bit_total, dtype=jnp.int32)
    offsets = jnp.left_shift(jnp.ones((ROUNDS - 1,), jnp.int32), bits)
    return jnp.bitwise_xor(jnp.arange(N_PAIR, dtype=jnp.int32)[None, :], offsets[:, None]).astype(jnp.int32)


def setup_inputs(seed: int = 0) -> dict:
    seeds = jax.random.split(jax.random.key(seed), 3)
    matrix = draw_matrix(jax.random.fold_in(seeds[2], 71), 0)
    partner = draw_partner(jax.random.fold_in(seeds[2], 71), 0)
    return {"matrix": matrix, "partner": partner}


def orthogonalizer(gram):
    identity = jnp.eye(gram.shape[0], dtype=jnp.float32)
    frobenius = jnp.sqrt(jnp.sum(gram * gram))
    square_root = gram / frobenius
    inverse_root = identity
    for step_count in range(NS_ITERS):
        correction = 1.5 * identity - 0.5 * jnp.dot(inverse_root, square_root, precision=lax.Precision.HIGHEST)
        square_root = jnp.dot(square_root, correction, precision=lax.Precision.HIGHEST)
        inverse_root = jnp.dot(correction, inverse_root, precision=lax.Precision.HIGHEST)
    return inverse_root * (jnp.sqrt(jnp.diagonal(gram)) / jnp.sqrt(frobenius))[None, :]

def reference(matrix, partner):
    blocks = matrix.reshape(ROWS, N_PAIR, 2 * B).transpose(1, 0, 2)
    for round_index in range(ROUNDS):
        gram = jnp.einsum('prc,prd->pcd', blocks, blocks, precision=lax.Precision.HIGHEST)
        rotation = jax.vmap(orthogonalizer)(gram)
        blocks = jnp.einsum('prc,pcd->prd', blocks, rotation, precision=lax.Precision.HIGHEST)
        if round_index + 1 < ROUNDS:
            second = blocks[:, :, B:][partner[round_index]]
            blocks = jnp.concatenate([blocks[:, :, :B], second], axis=2)
    return blocks.transpose(1, 0, 2).reshape(ROWS, 2 * B * N_PAIR)
```

```python
import functools

import jax
import jax.numpy as jnp
from jax import lax
from jax.experimental import pallas as pl
from jax.experimental.pallas import tpu as pltpu
from jax.sharding import PartitionSpec as P

ROUNDS = 4
NS_ITERS = 6
F32 = jnp.float32
BF16 = jnp.bfloat16
VMEM_LIMIT = 40 * 1024 * 1024


def split(x):
    high = x.astype(BF16)
    rest = x - high.astype(F32)
    mid = rest.astype(BF16)
    low = (rest - mid.astype(F32)).astype(BF16)
    return high, mid, low


def bdot(a, b, contract=((1,), (0,))):
    return lax.dot_general(a, b, (contract, ((), ())), preferred_element_type=F32)


def cat(*parts, axis=1):
    return jnp.concatenate(parts, axis=axis)


def pack_right(b):
    high, mid, low = split(b)
    wide = cat(high, mid)
    return cat(wide, wide, axis=0), cat(high, low, axis=0)


def dot_packed(a, packed):
    wide, narrow = packed
    n = narrow.shape[1]
    high, mid, low = split(a)
    main = bdot(cat(high, mid), wide)
    return main[:, :n] + (main[:, n:] + bdot(cat(low, high), narrow))


def dot(a, b):
    return dot_packed(a, pack_right(b))


def gram_of(x):
    high, mid, low = split(x)
    both = cat(high, mid)
    n = x.shape[1]
    main = bdot(both, both, ((0,), (0,)))
    edge = bdot(high, low, ((0,), (0,)))
    return main[:n, :n] + ((main[:n, n:] + main[n:, :n]) + (main[n:, n:] + (edge + edge.T)))


def orthogonalizers(grams):
    n = grams[0].shape[0]
    row = lax.broadcasted_iota(jnp.int32, (n, n), 0)
    col = lax.broadcasted_iota(jnp.int32, (n, n), 1)
    identity = jnp.where(row == col, 1.0, 0.0).astype(F32)
    norms = [jnp.sqrt(jnp.sum(g * g, keepdims=True)) for g in grams]
    products = [g / norm for g, norm in zip(grams, norms)]
    corrections = [1.5 * identity - 0.5 * w for w in products]
    roots = corrections
    for _ in range(NS_ITERS - 1):
        packed = [pack_right(m) for m in corrections]
        halves = [dot_packed(w, m) for w, m in zip(products, packed)]
        products = [dot_packed(t, m) for t, m in zip(halves, packed)]
        corrections = [1.5 * identity - 0.5 * w for w in products]
        roots = [dot(z, m) for z, m in zip(roots, corrections)]
    out = []
    for z, g, norm in zip(roots, grams, norms):
        diagonal = jnp.sum(jnp.where(row == col, g, 0.0), axis=0, keepdims=True)
        out.append(z * (jnp.sqrt(diagonal) / jnp.sqrt(norm)))
    return out


def total(refs):
    values = [ref[...] for ref in refs]
    while len(values) > 1:
        values = [sum(values[i : i + 2][1:], values[i]) for i in range(0, len(values), 2)]
    return values[0]


def vmem_call(kernel, outs, args, scratch=(), any_args=()):
    specs = [pl.BlockSpec(memory_space=pl.ANY if i in any_args else pltpu.VMEM) for i in range(len(args))]
    return pl.pallas_call(
        kernel,
        out_shape=[jax.ShapeDtypeStruct(shape, F32) for shape in outs],
        in_specs=specs,
        out_specs=[pl.BlockSpec(memory_space=pltpu.VMEM) for _ in outs],
        scratch_shapes=list(scratch),
        compiler_params=pltpu.CompilerParams(vmem_limit_bytes=VMEM_LIMIT),
    )(*args)


def gram_kernel(x_ref, gram_ref):
    gram_ref[...] = gram_of(x_ref[...])


def gram(x):
    width = x.shape[1]
    return vmem_call(gram_kernel, [(width, width)], [x])[0]


def merge_kernel(x_ref, folded_ref, merged_ref, gram_ref):
    half_rows, width = folded_ref.shape
    folded = folded_ref[...]
    second = lax.broadcasted_iota(jnp.int32, (half_rows, width), 1) >= width // 2
    top = jnp.where(second, pltpu.roll(folded, width // 2, 1), x_ref[:half_rows, :])
    bottom = jnp.where(second, folded, x_ref[half_rows:, :])
    merged_ref[:half_rows, :] = top
    merged_ref[half_rows:, :] = bottom
    gram_ref[...] = gram_of(top) + gram_of(bottom)


def merge(x, folded):
    width = x.shape[1]
    return vmem_call(merge_kernel, [x.shape, (width, width)], [x, folded])


def rotate_kernel(count, fold, x_hbm, *refs):
    parts, outs, (x_ref, sem) = refs[:count], refs[count:-2], refs[-2:]
    copy = pltpu.make_async_copy(x_hbm, x_ref, sem)
    copy.start()
    rotation = pack_right(orthogonalizers([total(parts)])[0])
    copy.wait()
    rows, width = x_ref.shape
    half = rows // 2
    top = dot_packed(x_ref[:half, :], rotation)
    bottom = dot_packed(x_ref[half:, :], rotation)
    outs[0][:half, :] = top
    outs[0][half:, :] = bottom
    if fold:
        second = lax.broadcasted_iota(jnp.int32, (half, width), 1) >= width // 2
        outs[1][...] = jnp.where(second, bottom, pltpu.roll(top, width // 2, 1))


def rotate(x, parts, fold):
    rows, width = x.shape
    outs = [x.shape] + ([(rows // 2, width)] if fold else [])
    return vmem_call(
        functools.partial(rotate_kernel, len(parts), fold),
        outs,
        [x, *parts],
        [pltpu.VMEM(x.shape, F32), pltpu.SemaphoreType.DMA],
        any_args=(0,),
    )


def swap(value, axis, mask):
    return lax.ppermute(value, axis, [(i, i ^ mask) for i in range(lax.axis_size(axis))])


def row_sum_parts(value):
    masks = [1 << bit for bit in range(lax.axis_size("row").bit_length() - 1)]
    parts = [value, swap(value, "row", masks[0])]
    for start in range(1, len(masks), 2):
        value = sum(parts[1:], parts[0])
        near = masks[start : start + 2]
        reach = near + ([near[0] ^ near[1]] if len(near) == 2 else [])
        parts = [value] + [swap(value, "row", mask) for mask in reach]
    return parts


def body(matrix, partner):
    bits = lax.axis_size("pair").bit_length() - 1
    me = lax.axis_index("pair")
    columns = matrix
    local = gram(columns)
    for index in range(ROUNDS):
        last = index + 1 == ROUNDS
        rotated = rotate(columns, row_sum_parts(local), not last)
        if last:
            return rotated[0]
        offset = jnp.bitwise_xor(partner[index, me], me)
        positions = jnp.arange(bits, dtype=jnp.int32)
        which = jnp.sum(jnp.bitwise_and(jnp.right_shift(offset, positions), 1) * positions)
        branches = [functools.partial(swap, axis="pair", mask=1 << bit) for bit in range(bits)]
        folded = lax.switch(which, branches, rotated[1])
        columns, local = merge(rotated[0], folded)


def solution(mesh):
    return jax.shard_map(
        body, mesh=mesh, in_specs=(P("row", "pair"), P()), out_specs=P("row", "pair"), check_vma=False
    )
```

```python
import functools

import jax
import jax.numpy as jnp
from jax import lax
from jax.experimental import pallas as pl
from jax.experimental.pallas import tpu as pltpu
from jax.sharding import PartitionSpec as P

ROUNDS = 4
NS_ITERS = 6
F32 = jnp.float32
BF16 = jnp.bfloat16
VMEM_LIMIT = 40 * 1024 * 1024
CHUNK = 512
ROWS_BY_ROWS = ((0,), (0,))


def split(x):
    high = x.astype(BF16)
    rest = x - high.astype(F32)
    mid = rest.astype(BF16)
    low = (rest - mid.astype(F32)).astype(BF16)
    return high, mid, low


def bdot(a, b, contract=((1,), (0,))):
    return lax.dot_general(a, b, (contract, ((), ())), preferred_element_type=F32)


def cat(*parts, axis=1):
    return jnp.concatenate(parts, axis=axis)


def pack_right(b):
    high, mid, low = split(b)
    wide = cat(high, mid)
    return cat(wide, wide, axis=0), cat(high, low, axis=0)


def dot_packed(a, packed):
    wide, narrow = packed
    n = narrow.shape[1]
    high, mid, low = split(a)
    main = bdot(cat(high, mid), wide)
    return main[:, :n] + (main[:, n:] + bdot(cat(low, high), narrow))


def dot(a, b):
    return dot_packed(a, pack_right(b))


def indices(n):
    return lax.broadcasted_iota(jnp.int32, (n, n), 0), lax.broadcasted_iota(jnp.int32, (n, n), 1)


def transform(gram, root, product, norm):
    row, col = indices(gram.shape[0])
    masked = jnp.where(row == col, gram, 0.0)
    root_norm = jnp.sqrt(norm)
    across = jnp.sqrt(jnp.sum(masked, axis=0, keepdims=True))
    down = jnp.sqrt(jnp.sum(masked, axis=1, keepdims=True))
    rotated = None if product is None else product * across * down
    return root * (across / root_norm), root * (down / root_norm), rotated


def orthogonalizers(grams, keep_going=False):
    row, col = indices(grams[0].shape[0])
    identity = jnp.where(row == col, 1.0, 0.0).astype(F32)
    norms = [jnp.sqrt(jnp.sum(g * g, keepdims=True)) for g in grams]

    def step(_, state):
        products, roots = state
        corrections = [pack_right(1.5 * identity - 0.5 * w) for w in products]
        halves = [dot_packed(w, m) for w, m in zip(products, corrections)]
        roots = [dot_packed(z, m) for z, m in zip(roots, corrections)]
        return [dot_packed(t, m) for t, m in zip(halves, corrections)], roots

    products = [g / norm for g, norm in zip(grams, norms)]
    state = products, [identity] * len(grams)
    products, roots = lax.fori_loop(0, NS_ITERS if keep_going else NS_ITERS - 1, step, state)
    if not keep_going:
        roots = [dot(z, 1.5 * identity - 0.5 * w) for z, w in zip(roots, products)]
        products = [None] * len(grams)
    return [transform(*args) for args in zip(grams, roots, products, norms)]


def total(values):
    while len(values) > 1:
        values = [sum(values[i + 1 : i + 2], values[i]) for i in range(0, len(values), 2)]
    return values[0]


def vmem_call(kernel, outs, args, scratch=(), places={}):
    return pl.pallas_call(
        kernel,
        out_shape=[jax.ShapeDtypeStruct(shape, F32) for shape in outs],
        in_specs=[pl.BlockSpec(memory_space=places.get(i, pltpu.VMEM)) for i in range(len(args))],
        out_specs=[pl.BlockSpec(memory_space=pltpu.VMEM) for _ in outs],
        scratch_shapes=list(scratch),
        compiler_params=pltpu.CompilerParams(vmem_limit_bytes=VMEM_LIMIT),
    )(*args)


def add_gram(x, main_ref, edge_ref):
    high, mid, low = split(x)
    both = cat(high, mid)
    main_ref[...] += bdot(both, both, ROWS_BY_ROWS)
    edge_ref[...] += bdot(high, low, ROWS_BY_ROWS)


def gram_total(main_ref, edge_ref):
    n = edge_ref.shape[1]
    main, edge = main_ref[...], edge_ref[...]
    return main[:n, :n] + ((main[:n, n:] + main[n:, :n]) + (main[n:, n:] + (edge + edge.T)))


def gram_scratch(width):
    return [pltpu.VMEM((2 * width, 2 * width), F32), pltpu.VMEM((width, width), F32)]


def clear(*refs):
    for ref in refs:
        ref[...] = jnp.zeros_like(ref)


def each_chunk(rows, step):
    lax.fori_loop(0, rows // CHUNK, lambda i, _: step(pl.multiple_of(i * CHUNK, CHUNK)), None)


def halves_kernel(upper, x_hbm, kept_ref, rest_ref, sems):
    half = kept_ref.shape[0]
    copies = [
        pltpu.make_async_copy(x_hbm.at[pl.ds(pl.multiple_of(at * half, half), half)], ref, sems.at[i])
        for i, (at, ref) in enumerate(((1 - upper[0], rest_ref), (upper[0], kept_ref)))
    ]
    for copy in copies:
        copy.start()
    for copy in copies:
        copy.wait()


def halves(upper, x):
    rows, width = x.shape
    return vmem_call(
        halves_kernel,
        [(rows // 2, width)] * 2,
        [upper, x],
        [pltpu.SemaphoreType.DMA((2,))],
        {0: pltpu.SMEM, 1: pl.ANY},
    )


def gram_kernel(kept_ref, rest_ref, gram_ref, *scratch):
    clear(*scratch)
    for ref in (kept_ref, rest_ref):
        add_gram(ref[...], *scratch)
    gram_ref[...] = gram_total(*scratch)


def gram(kept, rest):
    width = kept.shape[1]
    return vmem_call(gram_kernel, [(width, width)], [kept, rest], gram_scratch(width))[0]


def second_half(shape):
    return lax.broadcasted_iota(jnp.int32, shape, 1) >= shape[1] // 2


def merge_kernel(upper, x_ref, folded_ref, kept_ref, rest_ref, gram_ref, *scratch):
    half, width = folded_ref.shape
    second = second_half((CHUNK, width))
    clear(*scratch)

    def step(at):
        rows = pl.ds(at, CHUNK)
        folded = folded_ref[rows, :]
        top = jnp.where(second, pltpu.roll(folded, width // 2, 1), x_ref[rows, :])
        bottom = jnp.where(second, folded, x_ref[pl.ds(half + at, CHUNK), :])
        kept_ref[rows, :] = jnp.where(upper[0] == 1, bottom, top)
        rest_ref[rows, :] = jnp.where(upper[0] == 1, top, bottom)
        add_gram(cat(top, bottom, axis=0), *scratch)

    each_chunk(half, step)
    gram_ref[...] = gram_total(*scratch)


def merge(upper, x, folded):
    width = x.shape[1]
    outs = [folded.shape] * 2 + [(width, width)]
    return vmem_call(merge_kernel, outs, [upper, x, folded], gram_scratch(width), {0: pltpu.SMEM})


def write_rows(upper, sources, out_ref, folded_ref):
    half, width = sources[0][0].shape
    second = second_half((CHUNK, width))

    def step(at):
        rows = pl.ds(at, CHUNK)
        kept, rest = (
            total([dot_packed(pair[i][rows, :], packed) for *pair, packed in sources]) for i in range(2)
        )
        out_ref[pl.ds(pl.multiple_of(upper * half + at, CHUNK), CHUNK), :] = kept
        out_ref[pl.ds(pl.multiple_of((1 - upper) * half + at, CHUNK), CHUNK), :] = rest
        top, bottom = jnp.where(upper == 1, rest, kept), jnp.where(upper == 1, kept, rest)
        folded_ref[rows, :] = jnp.where(second, bottom, pltpu.roll(top, width // 2, 1))

    each_chunk(half, step)


def rows_call(kernel, args, kept):
    half, width = kept.shape
    return vmem_call(kernel, [(2 * half, width), kept.shape], args, places={0: pltpu.SMEM})


def rotate_kernel(count, upper, kept_ref, rest_ref, *refs):
    gram_sum = total([part[...] for part in refs[:count]])
    rotation = pack_right(orthogonalizers([gram_sum])[0][0])
    write_rows(upper[0], [(kept_ref, rest_ref, rotation)], *refs[count:])


def rotate(upper, kept, rest, parts):
    return rows_call(functools.partial(rotate_kernel, len(parts)), [upper, kept, rest, *parts], kept)


def cross_kernel(upper, own_ref, other_ref, gram_ref, sent_ref):
    n = own_ref.shape[1]
    high, mid, low = split(own_ref[...])
    other_high, other_mid, other_low = split(other_ref[...])
    main = bdot(cat(high, mid), cat(other_high, other_mid), ROWS_BY_ROWS)
    edge = bdot(high, other_low, ROWS_BY_ROWS) + bdot(low, other_high, ROWS_BY_ROWS)
    cross = main[:n, :n] + ((main[:n, n:] + main[n:, :n]) + (main[n:, n:] + edge))
    sent_ref[:n, :] = jnp.where(upper[0] == 1, cross.T, cross)
    sent_ref[n:, :] = gram_ref[...]


def cross_gram(upper, own, other, own_gram):
    width = own.shape[1]
    return vmem_call(cross_kernel, [(2 * width, width)], [upper, own, other, own_gram], places={0: pltpu.SMEM})[0]


def join_kernel(sent_ref, got_ref, own_ref, sum_ref, copy_ref):
    n = sum_ref.shape[0]
    sum_ref[...] = sent_ref[:n, :] + got_ref[:n, :]
    copy_ref[...] = own_ref[...]


def join(sent, got, own):
    return vmem_call(join_kernel, [(sent.shape[1],) * 2, own.shape], [sent, got, own])


def first_kernel(own_ref, other_ref, *outs):
    n = own_ref.shape[1]
    pair = orthogonalizers([own_ref[n:, :], other_ref[n:, :]], True)
    (outs[0][...], outs[1][...], outs[2][...]), (outs[3][...], _, outs[4][...]) = pair


def first_rotations(sent, got):
    return vmem_call(first_kernel, [(sent.shape[1],) * 2] * 5, [sent, got])


def run_kernel(count, upper, exchanges, v0, t0, g0, v1, g1, *refs):
    parts, (from_own, from_other) = refs[:count], refs[count:]
    n = v0.shape[0]
    row, col = indices(n)
    first_row, first_col = row < n // 2, col < n // 2

    def by_block(aa, ab, ba, bb):
        return jnp.where(first_row, jnp.where(first_col, aa, ab), jnp.where(first_col, ba, bb))

    def trade(own, other, cross, own_map, other_map):
        flipped = cross.T
        return (
            by_block(own, cross, flipped, other),
            by_block(other, flipped, cross, own),
            by_block(cross, own, other, flipped),
            [jnp.where(first_col, a, b) for a, b in zip(own_map, other_map)],
            [jnp.where(first_col, b, a) for a, b in zip(own_map, other_map)],
        )

    def step(_, state):
        own, other, cross, own_map, other_map = trade(*state)
        (v, t, own), (w, _, other) = orthogonalizers([own, other], True)
        v, w = pack_right(v), pack_right(w)
        cross = dot(t, dot_packed(cross, w))
        return own, other, cross, [dot_packed(m, v) for m in own_map], [dot_packed(m, w) for m in other_map]

    cross = total([part[...] for part in parts])
    cross = jnp.where(upper[0] == 1, cross.T, cross)
    cross = dot(t0[...], dot(cross, v1[...]))
    zeros = jnp.zeros((n, n), F32)
    state = g0[...], g1[...], cross, [v0[...], zeros], [zeros, v1[...]]
    from_own[...], from_other[...] = lax.fori_loop(0, exchanges[0], step, state)[3]


def run_maps(upper, exchanges, first, parts):
    args = [upper, exchanges, *first, *parts]
    outs = [parts[0].shape] * 2
    return vmem_call(functools.partial(run_kernel, len(parts)), outs, args, places={0: pltpu.SMEM, 1: pltpu.SMEM})


def apply_kernel(upper, kept, rest, kept_other, rest_other, from_own, from_other, *outs):
    own, other = pack_right(from_own[...]), pack_right(from_other[...])
    write_rows(upper[0], [(kept, rest, own), (kept_other, rest_other, other)], *outs)


def apply_maps(upper, own, other, maps):
    return rows_call(apply_kernel, [upper, *own, *other, *maps], own[0])


def swap(value, axis, mask):
    return lax.ppermute(value, axis, [(i, i ^ mask) for i in range(lax.axis_size(axis))])


def row_sum_parts(value):
    masks = [1 << bit for bit in range(lax.axis_size("row").bit_length() - 1)]
    parts = [value, swap(value, "row", masks[0])]
    for start in range(1, len(masks), 2):
        value = total(parts)
        near = masks[start : start + 2]
        reach = near + ([near[0] ^ near[1]] if len(near) == 2 else [])
        parts = [value] + [swap(value, "row", mask) for mask in reach]
    return parts


def by_stride(bit, function, *args):
    bits = lax.axis_size("pair").bit_length() - 1
    return lax.switch(bit, [functools.partial(function, 1 << b) for b in range(bits)], *args)


def exchange(bit, folded):
    return by_stride(bit, lambda mask, value: swap(value, "pair", mask), folded)


def upper_in(bit):
    return jnp.bitwise_and(jnp.right_shift(lax.axis_index("pair"), bit), 1).reshape(1)


def run(bit, upper, exchanges, kept, rest, local):
    mask = 1 << bit
    kept_other = swap(rest, "pair", mask)
    sent = cross_gram(upper, kept, kept_other, total(row_sum_parts(local)))
    got = swap(sent, "pair", mask)
    first = first_rotations(sent, got)
    cross, kept_again = join(sent, got, kept)
    rest_other = swap(kept_again, "pair", mask)
    maps = run_maps(upper, exchanges.reshape(1), first, row_sum_parts(cross))
    return apply_maps(upper, (kept, rest), (kept_other, rest_other), maps)


def one_round(upper, kept, rest, local):
    return rotate(upper, kept, rest, row_sum_parts(local))


def rounds(bit, matrix, early, late, exchanges, first, last):
    upper, zero = upper_in(bit), jnp.zeros((1,), jnp.int32)
    kept, rest = halves(upper, matrix)

    def lead(kept, rest, local):
        columns, folded = one_round(upper, kept, rest, local)
        return tuple(merge(upper, columns, exchange(first, folded)))

    def close(columns, folded):
        return one_round(zero, *merge(zero, columns, exchange(last, folded)))[0]

    state = lax.cond(early, lambda *state: state, lead, kept, rest, gram(kept, rest))
    columns, folded = run(bit, upper, exchanges, *state)
    return lax.cond(late, lambda columns, _: columns, close, columns, folded)


def body(matrix, partner):
    bits = lax.axis_size("pair").bit_length() - 1
    which = []
    for index in range(ROUNDS - 1):
        stride = partner[index, 0]
        which.append(sum(((stride >= 1 << bit).astype(jnp.int32) for bit in range(1, bits)), jnp.int32(0)))
    early, late = which[0] == which[1], which[1] == which[2]
    exchanges = 1 + early.astype(jnp.int32) + late.astype(jnp.int32)
    branches = [functools.partial(rounds, bit) for bit in range(bits)]
    return lax.switch(which[1], branches, matrix, early, late, exchanges, which[0], which[2])


def solution(mesh):
    return jax.shard_map(
        body, mesh=mesh, in_specs=(P("row", "pair"), P()), out_specs=P("row", "pair"), check_vma=False
    )
```

```python
import functools

import jax
import jax.numpy as jnp
from jax import lax
from jax.experimental import pallas as pl
from jax.experimental.pallas import tpu as pltpu
from jax.sharding import PartitionSpec as P

ROUNDS = 4
NS_ITERS = 6
F32 = jnp.float32
BF16 = jnp.bfloat16
VMEM_LIMIT = 40 * 1024 * 1024
CHUNK = 512
ROWS_BY_ROWS = ((0,), (0,))


def split(x):
    high = x.astype(BF16)
    rest = x - high.astype(F32)
    mid = rest.astype(BF16)
    low = (rest - mid.astype(F32)).astype(BF16)
    return high, mid, low


def bdot(a, b, contract=((1,), (0,))):
    return lax.dot_general(a, b, (contract, ((), ())), preferred_element_type=F32)


def cat(*parts, axis=1):
    return jnp.concatenate(parts, axis=axis)


def pack_right(b):
    high, mid, low = split(b)
    wide = cat(high, mid)
    return cat(wide, wide, axis=0), cat(high, low, axis=0)


def dot_packed(a, packed):
    wide, narrow = packed
    n = narrow.shape[1]
    high, mid, low = split(a)
    main = bdot(cat(high, mid), wide)
    return main[:, :n] + (main[:, n:] + bdot(cat(low, high), narrow))


def dot(a, b):
    return dot_packed(a, pack_right(b))


def indices(n):
    return lax.broadcasted_iota(jnp.int32, (n, n), 0), lax.broadcasted_iota(jnp.int32, (n, n), 1)


def transform(gram, root, product, norm):
    row, col = indices(gram.shape[0])
    masked = jnp.where(row == col, gram, 0.0)
    root_norm = jnp.sqrt(norm)
    across = jnp.sqrt(jnp.sum(masked, axis=0, keepdims=True))
    down = jnp.sqrt(jnp.sum(masked, axis=1, keepdims=True))
    rotated = None if product is None else product * across * down
    return root * (across / root_norm), root * (down / root_norm), rotated


def orthogonalizers(grams, keep_going=False):
    row, col = indices(grams[0].shape[0])
    identity = jnp.where(row == col, 1.0, 0.0).astype(F32)
    norms = [jnp.sqrt(jnp.sum(g * g, keepdims=True)) for g in grams]

    def step(_, state):
        products, roots = state
        corrections = [pack_right(1.5 * identity - 0.5 * w) for w in products]
        halves = [dot_packed(w, m) for w, m in zip(products, corrections)]
        roots = [dot_packed(z, m) for z, m in zip(roots, corrections)]
        return [dot_packed(t, m) for t, m in zip(halves, corrections)], roots

    products = [g / norm for g, norm in zip(grams, norms)]
    state = products, [identity] * len(grams)
    products, roots = lax.fori_loop(0, NS_ITERS if keep_going else NS_ITERS - 1, step, state)
    if not keep_going:
        roots = [dot(z, 1.5 * identity - 0.5 * w) for z, w in zip(roots, products)]
        products = [None] * len(grams)
    return [transform(*args) for args in zip(grams, roots, products, norms)]


def total(values):
    while len(values) > 1:
        values = [sum(values[i + 1 : i + 2], values[i]) for i in range(0, len(values), 2)]
    return values[0]


def vmem_call(kernel, outs, args, scratch=(), places={}):
    return pl.pallas_call(
        kernel,
        out_shape=[jax.ShapeDtypeStruct(shape, F32) for shape in outs],
        in_specs=[pl.BlockSpec(memory_space=places.get(i, pltpu.VMEM)) for i in range(len(args))],
        out_specs=[pl.BlockSpec(memory_space=pltpu.VMEM) for _ in outs],
        scratch_shapes=list(scratch),
        compiler_params=pltpu.CompilerParams(vmem_limit_bytes=VMEM_LIMIT),
    )(*args)


def add_gram(x, main_ref, edge_ref):
    high, mid, low = split(x)
    both = cat(high, mid)
    main_ref[...] += bdot(both, both, ROWS_BY_ROWS)
    edge_ref[...] += bdot(high, low, ROWS_BY_ROWS)


def gram_total(main_ref, edge_ref):
    n = edge_ref.shape[1]
    main, edge = main_ref[...], edge_ref[...]
    return main[:n, :n] + ((main[:n, n:] + main[n:, :n]) + (main[n:, n:] + (edge + edge.T)))


def gram_scratch(width):
    return [pltpu.VMEM((2 * width, 2 * width), F32), pltpu.VMEM((width, width), F32)]


def clear(*refs):
    for ref in refs:
        ref[...] = jnp.zeros_like(ref)


def each_chunk(rows, step):
    lax.fori_loop(0, rows // CHUNK, lambda i, _: step(pl.multiple_of(i * CHUNK, CHUNK)), None)


def scalars_kernel(bits, partner, place, first, middle, last, lead, closing, exchanges):
    strides = [partner[index, 0] for index in range(ROUNDS - 1)]
    zero = jnp.int32(0)
    which = [sum(((s >= 1 << bit).astype(jnp.int32) for bit in range(1, bits)), zero) for s in strides]
    first[0], middle[0], last[0] = which
    early, late = (which[0] == which[1]).astype(jnp.int32), (which[1] == which[2]).astype(jnp.int32)
    leap = jnp.where(which[0] < which[1], 1 - late, 0)
    place[0] = jnp.where(leap == 1, which[0], which[1])
    lead[0] = 1 - early - leap
    closing[0] = 1 - late + leap
    exchanges[...] = jnp.full(exchanges.shape, 1 + early + late, jnp.int32)


def pair_bits():
    return lax.axis_size("pair").bit_length() - 1


def scalars(partner):
    space = pl.BlockSpec(memory_space=pltpu.SMEM)
    return pl.pallas_call(
        functools.partial(scalars_kernel, pair_bits()),
        out_shape=[jax.ShapeDtypeStruct((1,), jnp.int32)] * 6 + [jax.ShapeDtypeStruct((8, 128), jnp.int32)],
        in_specs=[space],
        out_specs=[space] * 6 + [pl.BlockSpec(memory_space=pltpu.VMEM)],
    )(partner)


def upper_in(bit):
    return 0 if bit is None else jnp.bitwise_and(jnp.right_shift(lax.axis_index("pair"), bit), 1)


def halves_kernel(bit, x_hbm, kept_ref, rest_ref, sems):
    half, upper = kept_ref.shape[0], upper_in(bit)
    copies = [
        pltpu.make_async_copy(x_hbm.at[pl.ds(pl.multiple_of(at * half, half), half)], ref, sems.at[i])
        for i, (at, ref) in enumerate(((1 - upper, rest_ref), (upper, kept_ref)))
    ]
    for copy in copies:
        copy.start()
    for copy in copies:
        copy.wait()


def halves(bit, x):
    rows, width = x.shape
    outs = [(rows // 2, width)] * 2
    scratch = [pltpu.SemaphoreType.DMA((2,))]
    return vmem_call(functools.partial(halves_kernel, bit), outs, [x], scratch, {0: pl.ANY})


def gram_kernel(kept_ref, rest_ref, gram_ref, *scratch):
    clear(*scratch)
    for ref in (kept_ref, rest_ref):
        add_gram(ref[...], *scratch)
    gram_ref[...] = gram_total(*scratch)


def gram(kept, rest):
    width = kept.shape[1]
    return vmem_call(gram_kernel, [(width, width)], [kept, rest], gram_scratch(width))[0]


def in_order(upper, a, b):
    return (jnp.where(upper == 1, b, a), jnp.where(upper == 1, a, b)) if isinstance(upper, jax.Array) else (a, b)


def second_half(shape):
    return lax.broadcasted_iota(jnp.int32, shape, 1) >= shape[1] // 2


def merge_kernel(bit, x_ref, folded_ref, kept_ref, rest_ref, gram_ref, *scratch):
    half, width = folded_ref.shape
    second, upper = second_half((CHUNK, width)), upper_in(bit)
    clear(*scratch)

    def step(at):
        rows = pl.ds(at, CHUNK)
        folded = folded_ref[rows, :]
        top = jnp.where(second, pltpu.roll(folded, width // 2, 1), x_ref[rows, :])
        bottom = jnp.where(second, folded, x_ref[pl.ds(half + at, CHUNK), :])
        kept_ref[rows, :], rest_ref[rows, :] = in_order(upper, top, bottom)
        add_gram(cat(top, bottom, axis=0), *scratch)

    each_chunk(half, step)
    gram_ref[...] = gram_total(*scratch)


def merge(bit, x, folded):
    width = x.shape[1]
    outs = [folded.shape] * 2 + [(width, width)]
    return vmem_call(functools.partial(merge_kernel, bit), outs, [x, folded], gram_scratch(width))


def write_rows(upper, sources, out_ref, folded_ref=None):
    half, width = sources[0][0].shape
    second = second_half((CHUNK, width))

    def step(at):
        rows = pl.ds(at, CHUNK)
        kept, rest = (
            total([dot_packed(pair[i][rows, :], packed) for *pair, packed in sources]) for i in range(2)
        )
        out_ref[pl.ds(pl.multiple_of(upper * half + at, CHUNK), CHUNK), :] = kept
        out_ref[pl.ds(pl.multiple_of((1 - upper) * half + at, CHUNK), CHUNK), :] = rest
        if folded_ref is None:
            return
        top, bottom = in_order(upper, kept, rest)
        folded_ref[rows, :] = jnp.where(second, bottom, pltpu.roll(top, width // 2, 1))

    each_chunk(half, step)


def rows_call(kernel, args, kept, fold=True):
    half, width = kept.shape
    return vmem_call(kernel, [(2 * half, width)] + [kept.shape] * fold, args)


def rotate_kernel(bit, count, kept_ref, rest_ref, *refs):
    gram_sum = total([part[...] for part in refs[:count]])
    rotation = pack_right(orthogonalizers([gram_sum])[0][0])
    write_rows(upper_in(bit), [(kept_ref, rest_ref, rotation)], *refs[count:])


def rotate(bit, kept, rest, parts, fold):
    kernel = functools.partial(rotate_kernel, bit, len(parts))
    return rows_call(kernel, [kept, rest, *parts], kept, fold)


def cross_kernel(bit, own_ref, other_ref, gram_ref, sent_ref):
    n = own_ref.shape[1]
    high, mid, low = split(own_ref[...])
    other_high, other_mid, other_low = split(other_ref[...])
    main = bdot(cat(high, mid), cat(other_high, other_mid), ROWS_BY_ROWS)
    edge = bdot(high, other_low, ROWS_BY_ROWS) + bdot(low, other_high, ROWS_BY_ROWS)
    cross = main[:n, :n] + ((main[:n, n:] + main[n:, :n]) + (main[n:, n:] + edge))
    sent_ref[:n, :] = jnp.where(upper_in(bit) == 1, cross.T, cross)
    sent_ref[n:, :] = gram_ref[...]


def cross_gram(bit, own, other, own_gram):
    width = own.shape[1]
    return vmem_call(functools.partial(cross_kernel, bit), [(2 * width, width)], [own, other, own_gram])[0]


def join_kernel(sent_ref, got_ref, own_ref, sum_ref, copy_ref):
    n = sum_ref.shape[0]
    sum_ref[...] = sent_ref[:n, :] + got_ref[:n, :]
    copy_ref[...] = own_ref[...]


def join(sent, got, own):
    return vmem_call(join_kernel, [(sent.shape[1],) * 2, own.shape], [sent, got, own])


def first_kernel(own_ref, other_ref, *outs):
    n = own_ref.shape[1]
    pair = orthogonalizers([own_ref[n:, :], other_ref[n:, :]], True)
    (outs[0][...], outs[1][...], outs[2][...]), (outs[3][...], _, outs[4][...]) = pair


def first_rotations(sent, got):
    return vmem_call(first_kernel, [(sent.shape[1],) * 2] * 5, [sent, got])


def run_kernel(count, bit, exchanges, v0, t0, g0, v1, g1, *refs):
    parts, (from_own, from_other) = refs[:count], refs[count:]
    n = v0.shape[0]
    row, col = indices(n)
    first_row, first_col = row < n // 2, col < n // 2

    def by_block(aa, ab, ba, bb):
        return jnp.where(first_row, jnp.where(first_col, aa, ab), jnp.where(first_col, ba, bb))

    def trade(own, other, cross, own_map, other_map):
        flipped = cross.T
        return (
            by_block(own, cross, flipped, other),
            by_block(other, flipped, cross, own),
            by_block(cross, own, other, flipped),
            [jnp.where(first_col, a, b) for a, b in zip(own_map, other_map)],
            [jnp.where(first_col, b, a) for a, b in zip(own_map, other_map)],
        )

    def step(_, state):
        own, other, cross, own_map, other_map = trade(*state)
        (v, t, own), (w, _, other) = orthogonalizers([own, other], True)
        v, w = pack_right(v), pack_right(w)
        cross = dot(t, dot_packed(cross, w))
        return own, other, cross, [dot_packed(m, v) for m in own_map], [dot_packed(m, w) for m in other_map]

    cross = total([part[...] for part in parts])
    cross = jnp.where(upper_in(bit) == 1, cross.T, cross)
    cross = dot(t0[...], dot(cross, v1[...]))
    zeros = jnp.zeros((n, n), F32)
    state = g0[...], g1[...], cross, [v0[...], zeros], [zeros, v1[...]]
    from_own[...], from_other[...] = lax.fori_loop(0, jnp.max(exchanges[...]), step, state)[3]


def run_maps(bit, exchanges, first, parts):
    args = [exchanges, *first, *parts]
    outs = [parts[0].shape] * 2
    return vmem_call(functools.partial(run_kernel, len(parts), bit), outs, args)


def apply_kernel(bit, kept, rest, kept_other, rest_other, from_own, from_other, *outs):
    own, other = pack_right(from_own[...]), pack_right(from_other[...])
    write_rows(upper_in(bit), [(kept, rest, own), (kept_other, rest_other, other)], *outs)


def apply_maps(bit, kept, rest, kept_other, rest_other, maps):
    return rows_call(functools.partial(apply_kernel, bit), [kept, rest, kept_other, rest_other, *maps], kept)


def swap(value, axis, mask):
    return lax.ppermute(value, axis, [(i, i ^ mask) for i in range(lax.axis_size(axis))])


def row_sum_parts(value):
    masks = [1 << bit for bit in range(lax.axis_size("row").bit_length() - 1)]
    parts = [value, swap(value, "row", masks[0])]
    for start in range(1, len(masks), 2):
        value = total(parts)
        near = masks[start : start + 2]
        reach = ([near[0] ^ near[1]] if len(near) == 2 else []) + near
        parts = [value] + [swap(value, "row", mask) for mask in reach]
    return parts


def pair_swap(mask, value):
    return swap(value, "pair", mask)


def by_stride(bit, function, *args):
    return lax.switch(bit, [functools.partial(function, 1 << b) for b in range(pair_bits())], *args)


def run(bit, exchanges, kept, rest, local):
    mask = 1 << bit
    kept_other = swap(rest, "pair", mask)
    own_gram = total(row_sum_parts(local))
    sent = cross_gram(bit, kept, kept_other, own_gram)
    got = swap(sent, "pair", mask)
    cross, kept_again = join(sent, got, kept)
    rest_other = swap(kept_again, "pair", mask)
    first = first_rotations(sent, got)
    maps = run_maps(bit, exchanges, first, row_sum_parts(cross))
    return apply_maps(bit, kept, rest, kept_other, rest_other, maps)


def one_round(bit, kept, rest, local, fold=True):
    return rotate(bit, kept, rest, row_sum_parts(local), fold)


def rounds(bit, matrix, first, middle, last, lead, closing, exchanges):
    kept, rest = halves(bit, matrix)

    def go_ahead(kept, rest, local):
        columns, folded = one_round(bit, kept, rest, local)
        return tuple(merge(bit, columns, by_stride(first[0], pair_swap, folded)))

    def follow(which, fold, columns, folded):
        return one_round(None, *merge(None, columns, by_stride(which[0], pair_swap, folded)), fold)

    def close(columns, folded):
        if bit + 1 < pair_bits():
            more = functools.partial(follow, middle, True)
            columns, folded = lax.cond(
                closing[0] == 2, lambda *args: tuple(more(*args)), lambda *args: args, columns, folded
            )
        return follow(last, False, columns, folded)[0]

    state = lax.cond(lead[0] == 1, go_ahead, lambda *state: state, kept, rest, gram(kept, rest))
    columns, folded = run(bit, exchanges, *state)
    return lax.cond(closing[0] == 0, lambda columns, _: columns, close, columns, folded)


def body(matrix, partner):
    place, *others = scalars(partner)
    branches = [functools.partial(rounds, bit) for bit in range(pair_bits())]
    return lax.switch(place[0], branches, matrix, *others)


def solution(mesh):
    return jax.shard_map(
        body, mesh=mesh, in_specs=(P("row", "pair"), P()), out_specs=P("row", "pair"), check_vma=False
    )
```

```python
import functools

import jax
import jax.numpy as jnp
from jax import lax
from jax.experimental import pallas as pl
from jax.experimental.pallas import tpu as pltpu
from jax.sharding import PartitionSpec as P

ROUNDS = 4
NS_ITERS = 6
F32 = jnp.float32
BF16 = jnp.bfloat16
VMEM_LIMIT = 40 * 1024 * 1024
CHUNK = 512
ROWS_BY_ROWS = ((0,), (0,))


def split(x):
    high = x.astype(BF16)
    rest = x - high.astype(F32)
    mid = rest.astype(BF16)
    low = (rest - mid.astype(F32)).astype(BF16)
    return high, mid, low


def bdot(a, b, contract=((1,), (0,))):
    return lax.dot_general(a, b, (contract, ((), ())), preferred_element_type=F32)


def cat(*parts, axis=1):
    return jnp.concatenate(parts, axis=axis)


def pack_right(b):
    high, mid, low = split(b)
    wide = cat(high, mid)
    return cat(wide, wide, axis=0), cat(high, low, axis=0)


def dot_packed(a, packed):
    wide, narrow = packed
    n = narrow.shape[1]
    high, mid, low = split(a)
    main = bdot(cat(high, mid), wide)
    return main[:, :n] + (main[:, n:] + bdot(cat(low, high), narrow))


def dot(a, b):
    return dot_packed(a, pack_right(b))


def indices(n):
    return lax.broadcasted_iota(jnp.int32, (n, n), 0), lax.broadcasted_iota(jnp.int32, (n, n), 1)


def transform(gram, root, product, norm):
    row, col = indices(gram.shape[0])
    masked = jnp.where(row == col, gram, 0.0)
    root_norm = jnp.sqrt(norm)
    across = jnp.sqrt(jnp.sum(masked, axis=0, keepdims=True))
    down = jnp.sqrt(jnp.sum(masked, axis=1, keepdims=True))
    rotated = None if product is None else product * across * down
    return root * (across / root_norm), root * (down / root_norm), rotated


def orthogonalizers(grams, keep_going=False):
    row, col = indices(grams[0].shape[0])
    identity = jnp.where(row == col, 1.0, 0.0).astype(F32)
    norms = [jnp.sqrt(jnp.sum(g * g, keepdims=True)) for g in grams]

    def step(_, state):
        products, roots = state
        corrections = [pack_right(1.5 * identity - 0.5 * w) for w in products]
        halves = [dot_packed(w, m) for w, m in zip(products, corrections)]
        roots = [dot_packed(z, m) for z, m in zip(roots, corrections)]
        return [dot_packed(t, m) for t, m in zip(halves, corrections)], roots

    products = [g / norm for g, norm in zip(grams, norms)]
    state = products, [identity] * len(grams)
    products, roots = lax.fori_loop(0, NS_ITERS if keep_going else NS_ITERS - 1, step, state)
    if not keep_going:
        roots = [dot(z, 1.5 * identity - 0.5 * w) for z, w in zip(roots, products)]
        products = [None] * len(grams)
    return [transform(*args) for args in zip(grams, roots, products, norms)]


def total(values):
    while len(values) > 1:
        values = [sum(values[i + 1 : i + 2], values[i]) for i in range(0, len(values), 2)]
    return values[0]


def vmem_call(kernel, outs, args, scratch=(), places={}):
    return pl.pallas_call(
        kernel,
        out_shape=[jax.ShapeDtypeStruct(shape, F32) for shape in outs],
        in_specs=[pl.BlockSpec(memory_space=places.get(i, pltpu.VMEM)) for i in range(len(args))],
        out_specs=[pl.BlockSpec(memory_space=pltpu.VMEM) for _ in outs],
        scratch_shapes=list(scratch),
        compiler_params=pltpu.CompilerParams(vmem_limit_bytes=VMEM_LIMIT),
    )(*args)


def add_gram(x, main_ref, edge_ref):
    high, mid, low = split(x)
    both = cat(high, mid)
    main_ref[...] += bdot(both, both, ROWS_BY_ROWS)
    edge_ref[...] += bdot(high, low, ROWS_BY_ROWS)


def gram_total(main_ref, edge_ref):
    n = edge_ref.shape[1]
    main, edge = main_ref[...], edge_ref[...]
    return main[:n, :n] + ((main[:n, n:] + main[n:, :n]) + (main[n:, n:] + (edge + edge.T)))


def gram_scratch(width):
    return [pltpu.VMEM((2 * width, 2 * width), F32), pltpu.VMEM((width, width), F32)]


def clear(*refs):
    for ref in refs:
        ref[...] = jnp.zeros_like(ref)


def each_chunk(rows, step):
    lax.fori_loop(0, rows // CHUNK, lambda i, _: step(pl.multiple_of(i * CHUNK, CHUNK)), None)


def scalars_kernel(bits, partner, place, first, middle, last, lead, closing, exchanges):
    strides = [partner[index, 0] for index in range(ROUNDS - 1)]
    zero = jnp.int32(0)
    which = [sum(((s >= 1 << bit).astype(jnp.int32) for bit in range(1, bits)), zero) for s in strides]
    first[0], middle[0], last[0] = which
    early, late = (which[0] == which[1]).astype(jnp.int32), (which[1] == which[2]).astype(jnp.int32)
    leap = jnp.where(which[0] < which[1], 1 - late, 0)
    place[0] = jnp.where(leap == 1, which[0], which[1])
    lead[0] = 1 - early - leap
    closing[0] = 1 - late + leap
    exchanges[...] = jnp.full(exchanges.shape, 1 + early + late, jnp.int32)


def pair_bits():
    return lax.axis_size("pair").bit_length() - 1


def scalars(partner):
    space = pl.BlockSpec(memory_space=pltpu.SMEM)
    return pl.pallas_call(
        functools.partial(scalars_kernel, pair_bits()),
        out_shape=[jax.ShapeDtypeStruct((1,), jnp.int32)] * 6 + [jax.ShapeDtypeStruct((8, 128), jnp.int32)],
        in_specs=[space],
        out_specs=[space] * 6 + [pl.BlockSpec(memory_space=pltpu.VMEM)],
    )(partner)


def upper_in(bit):
    return 0 if bit is None else jnp.bitwise_and(jnp.right_shift(lax.axis_index("pair"), bit), 1)


def halves_kernel(bit, x_hbm, kept_ref, rest_ref, sems):
    half, upper = kept_ref.shape[0], upper_in(bit)
    copies = [
        pltpu.make_async_copy(x_hbm.at[pl.ds(pl.multiple_of(at * half, half), half)], ref, sems.at[i])
        for i, (at, ref) in enumerate(((1 - upper, rest_ref), (upper, kept_ref)))
    ]
    for copy in copies:
        copy.start()
    for copy in copies:
        copy.wait()


def halves(bit, x):
    rows, width = x.shape
    outs = [(rows // 2, width)] * 2
    scratch = [pltpu.SemaphoreType.DMA((2,))]
    return vmem_call(functools.partial(halves_kernel, bit), outs, [x], scratch, {0: pl.ANY})


def gram_kernel(kept_ref, rest_ref, gram_ref, *scratch):
    clear(*scratch)
    for ref in (kept_ref, rest_ref):
        add_gram(ref[...], *scratch)
    gram_ref[...] = gram_total(*scratch)


def gram(kept, rest):
    width = kept.shape[1]
    return vmem_call(gram_kernel, [(width, width)], [kept, rest], gram_scratch(width))[0]


def in_order(upper, a, b):
    return (jnp.where(upper == 1, b, a), jnp.where(upper == 1, a, b)) if isinstance(upper, jax.Array) else (a, b)


def second_half(shape):
    return lax.broadcasted_iota(jnp.int32, shape, 1) >= shape[1] // 2


def merge_kernel(bit, x_ref, folded_ref, kept_ref, rest_ref, *refs):
    half, width = folded_ref.shape
    second, upper = second_half((CHUNK, width)), upper_in(bit)
    clear(*refs[1:])

    def step(at):
        rows = pl.ds(at, CHUNK)
        folded = folded_ref[rows, :]
        top = jnp.where(second, pltpu.roll(folded, width // 2, 1), x_ref[rows, :])
        bottom = jnp.where(second, folded, x_ref[pl.ds(half + at, CHUNK), :])
        kept_ref[rows, :], rest_ref[rows, :] = in_order(upper, top, bottom)
        if refs:
            add_gram(cat(top, bottom, axis=0), *refs[1:])

    each_chunk(half, step)
    if refs:
        refs[0][...] = gram_total(*refs[1:])


def merge(bit, x, folded, with_gram=True):
    width = x.shape[1]
    outs = [folded.shape] * 2 + [(width, width)] * with_gram
    scratch = gram_scratch(width) if with_gram else []
    return vmem_call(functools.partial(merge_kernel, bit), outs, [x, folded], scratch)


def write_rows(upper, sources, out_ref, folded_ref=None):
    half, width = sources[0][0].shape
    second = second_half((CHUNK, width))

    def step(at):
        rows = pl.ds(at, CHUNK)
        kept, rest = (
            total([dot_packed(pair[i][rows, :], packed) for *pair, packed in sources]) for i in range(2)
        )
        out_ref[pl.ds(pl.multiple_of(upper * half + at, CHUNK), CHUNK), :] = kept
        out_ref[pl.ds(pl.multiple_of((1 - upper) * half + at, CHUNK), CHUNK), :] = rest
        if folded_ref is None:
            return
        top, bottom = in_order(upper, kept, rest)
        folded_ref[rows, :] = jnp.where(second, bottom, pltpu.roll(top, width // 2, 1))

    each_chunk(half, step)


def rows_call(kernel, args, kept, fold=True):
    half, width = kept.shape
    return vmem_call(kernel, [(2 * half, width)] + [kept.shape] * fold, args)


def rotate_kernel(bit, count, kept_ref, rest_ref, *refs):
    gram_sum = total([part[...] for part in refs[:count]])
    rotation = pack_right(orthogonalizers([gram_sum])[0][0])
    write_rows(upper_in(bit), [(kept_ref, rest_ref, rotation)], *refs[count:])


def rotate(bit, kept, rest, parts, fold):
    kernel = functools.partial(rotate_kernel, bit, len(parts))
    return rows_call(kernel, [kept, rest, *parts], kept, fold)


def cross_kernel(bit, own_ref, other_ref, gram_ref, sent_ref):
    n = own_ref.shape[1]
    high, mid, low = split(own_ref[...])
    other_high, other_mid, other_low = split(other_ref[...])
    main = bdot(cat(high, mid), cat(other_high, other_mid), ROWS_BY_ROWS)
    edge = bdot(high, other_low, ROWS_BY_ROWS) + bdot(low, other_high, ROWS_BY_ROWS)
    cross = main[:n, :n] + ((main[:n, n:] + main[n:, :n]) + (main[n:, n:] + edge))
    sent_ref[:n, :] = jnp.where(upper_in(bit) == 1, cross.T, cross)
    sent_ref[n:, :] = gram_ref[...]


def cross_gram(bit, own, other, own_gram):
    width = own.shape[1]
    return vmem_call(functools.partial(cross_kernel, bit), [(2 * width, width)], [own, other, own_gram])[0]


def join_kernel(sent_ref, got_ref, own_ref, sum_ref, copy_ref):
    n = sum_ref.shape[0]
    sum_ref[...] = sent_ref[:n, :] + got_ref[:n, :]
    copy_ref[...] = own_ref[...]


def join(sent, got, own):
    return vmem_call(join_kernel, [(sent.shape[1],) * 2, own.shape], [sent, got, own])


def first_kernel(own_ref, other_ref, *outs):
    n = own_ref.shape[1]
    pair = orthogonalizers([own_ref[n:, :], other_ref[n:, :]], True)
    (outs[0][...], outs[1][...], outs[2][...]), (outs[3][...], _, outs[4][...]) = pair


def first_rotations(sent, got):
    return vmem_call(first_kernel, [(sent.shape[1],) * 2] * 5, [sent, got])


def run_kernel(count, bit, exchanges, v0, t0, g0, v1, g1, *refs):
    parts, (from_own, from_other) = refs[:count], refs[count:]
    n = v0.shape[0]
    row, col = indices(n)
    first_row, first_col = row < n // 2, col < n // 2

    def by_block(aa, ab, ba, bb):
        return jnp.where(first_row, jnp.where(first_col, aa, ab), jnp.where(first_col, ba, bb))

    def trade(own, other, cross, own_map, other_map):
        flipped = cross.T
        return (
            by_block(own, cross, flipped, other),
            by_block(other, flipped, cross, own),
            by_block(cross, own, other, flipped),
            [jnp.where(first_col, a, b) for a, b in zip(own_map, other_map)],
            [jnp.where(first_col, b, a) for a, b in zip(own_map, other_map)],
        )

    def step(_, state):
        own, other, cross, own_map, other_map = trade(*state)
        (v, t, own), (w, _, other) = orthogonalizers([own, other], True)
        v, w = pack_right(v), pack_right(w)
        cross = dot(t, dot_packed(cross, w))
        return own, other, cross, [dot_packed(m, v) for m in own_map], [dot_packed(m, w) for m in other_map]

    cross = total([part[...] for part in parts])
    cross = jnp.where(upper_in(bit) == 1, cross.T, cross)
    cross = dot(t0[...], dot(cross, v1[...]))
    zeros = jnp.zeros((n, n), F32)
    state = g0[...], g1[...], cross, [v0[...], zeros], [zeros, v1[...]]
    from_own[...], from_other[...] = lax.fori_loop(0, jnp.max(exchanges[...]), step, state)[3]


def run_maps(bit, exchanges, first, parts):
    args = [exchanges, *first, *parts]
    outs = [parts[0].shape] * 2
    return vmem_call(functools.partial(run_kernel, len(parts), bit), outs, args)


def apply_kernel(bit, kept, rest, kept_other, rest_other, from_own, from_other, *outs):
    own, other = pack_right(from_own[...]), pack_right(from_other[...])
    write_rows(upper_in(bit), [(kept, rest, own), (kept_other, rest_other, other)], *outs)


def apply_maps(bit, kept, rest, kept_other, rest_other, maps):
    return rows_call(functools.partial(apply_kernel, bit), [kept, rest, kept_other, rest_other, *maps], kept)


def swap(value, axis, mask):
    return lax.ppermute(value, axis, [(i, i ^ mask) for i in range(lax.axis_size(axis))])


def row_sum_parts(value):
    masks = [1 << bit for bit in range(lax.axis_size("row").bit_length() - 1)]
    parts = [value, swap(value, "row", masks[0])]
    for start in range(1, len(masks), 2):
        value = total(parts)
        near = masks[start : start + 2]
        reach = ([near[0] ^ near[1]] if len(near) == 2 else []) + near
        parts = [value] + [swap(value, "row", mask) for mask in reach]
    return parts


def pair_swap(mask, value):
    return swap(value, "pair", mask)


def by_stride(bit, function, *args):
    return lax.switch(bit, [functools.partial(function, 1 << b) for b in range(pair_bits())], *args)


def run(bit, exchanges, kept, rest):
    mask = 1 << bit
    kept_other = swap(rest, "pair", mask)
    own_gram = total(row_sum_parts(gram(kept, rest)))
    sent = cross_gram(bit, kept, kept_other, own_gram)
    got = swap(sent, "pair", mask)
    cross, kept_again = join(sent, got, kept)
    rest_other = swap(kept_again, "pair", mask)
    first = first_rotations(sent, got)
    maps = run_maps(bit, exchanges, first, row_sum_parts(cross))
    return apply_maps(bit, kept, rest, kept_other, rest_other, maps)


def one_round(bit, kept, rest, local, fold=True):
    return rotate(bit, kept, rest, row_sum_parts(local), fold)


def rounds(bit, matrix, first, middle, last, lead, closing, exchanges):
    kept, rest = halves(bit, matrix)

    def go_ahead(kept, rest):
        columns, folded = one_round(bit, kept, rest, gram(kept, rest))
        return tuple(merge(bit, columns, by_stride(first[0], pair_swap, folded), False))

    def follow(which, fold, columns, folded):
        return one_round(None, *merge(None, columns, by_stride(which[0], pair_swap, folded)), fold)

    def close(columns, folded):
        if bit + 1 < pair_bits():
            more = functools.partial(follow, middle, True)
            columns, folded = lax.cond(
                closing[0] == 2, lambda *args: tuple(more(*args)), lambda *args: args, columns, folded
            )
        return follow(last, False, columns, folded)[0]

    state = lax.cond(lead[0] == 1, go_ahead, lambda *state: state, kept, rest)
    columns, folded = run(bit, exchanges, *state)
    return lax.cond(closing[0] == 0, lambda columns, _: columns, close, columns, folded)


def body(matrix, partner):
    place, *others = scalars(partner)
    branches = [functools.partial(rounds, bit) for bit in range(pair_bits())]
    return lax.switch(place[0], branches, matrix, *others)


def solution(mesh):
    return jax.shard_map(
        body, mesh=mesh, in_specs=(P("row", "pair"), P()), out_specs=P("row", "pair"), check_vma=False
    )
```

```python
import functools

import jax
import jax.numpy as jnp
from jax import lax
from jax.experimental import pallas as pl
from jax.experimental.pallas import tpu as pltpu
from jax.sharding import PartitionSpec as P

ROUNDS = 4
NS_ITERS = 6
F32 = jnp.float32
BF16 = jnp.bfloat16
VMEM_LIMIT = 40 * 1024 * 1024
CHUNK = 512
ROWS_BY_ROWS = ((0,), (0,))


def split(x):
    high = x.astype(BF16)
    rest = x - high.astype(F32)
    mid = rest.astype(BF16)
    low = (rest - mid.astype(F32)).astype(BF16)
    return high, mid, low


def bdot(a, b, contract=((1,), (0,))):
    return lax.dot_general(a, b, (contract, ((), ())), preferred_element_type=F32)


def cat(*parts, axis=1):
    return jnp.concatenate(parts, axis=axis)


def pack_right(b):
    high, mid, low = split(b)
    wide = cat(high, mid)
    return cat(wide, wide, axis=0), cat(high, low, axis=0)


def dot_packed(a, packed):
    wide, narrow = packed
    n = narrow.shape[1]
    high, mid, low = split(a)
    main = bdot(cat(high, mid), wide)
    return main[:, :n] + (main[:, n:] + bdot(cat(low, high), narrow))


def dot(a, b):
    return dot_packed(a, pack_right(b))


def indices(n):
    return lax.broadcasted_iota(jnp.int32, (n, n), 0), lax.broadcasted_iota(jnp.int32, (n, n), 1)


def transform(gram, root, product, norm):
    row, col = indices(gram.shape[0])
    masked = jnp.where(row == col, gram, 0.0)
    root_norm = jnp.sqrt(norm)
    across = jnp.sqrt(jnp.sum(masked, axis=0, keepdims=True))
    down = jnp.sqrt(jnp.sum(masked, axis=1, keepdims=True))
    rotated = None if product is None else product * across * down
    return root * (across / root_norm), root * (down / root_norm), rotated


def orthogonalizers(grams, keep_going=False, unroll=1):
    row, col = indices(grams[0].shape[0])
    identity = jnp.where(row == col, 1.0, 0.0).astype(F32)
    norms = [jnp.sqrt(jnp.sum(g * g, keepdims=True)) for g in grams]

    def step(_, state):
        products, roots = state
        corrections = [pack_right(1.5 * identity - 0.5 * w) for w in products]
        halves = [dot_packed(w, m) for w, m in zip(products, corrections)]
        roots = [dot_packed(z, m) for z, m in zip(roots, corrections)]
        return [dot_packed(t, m) for t, m in zip(halves, corrections)], roots

    products = [g / norm for g, norm in zip(grams, norms)]
    state = products, [identity] * len(grams)
    products, roots = lax.fori_loop(0, NS_ITERS if keep_going else NS_ITERS - 1, step, state, unroll=unroll)
    if not keep_going:
        roots = [dot(z, 1.5 * identity - 0.5 * w) for z, w in zip(roots, products)]
        products = [None] * len(grams)
    return [transform(*args) for args in zip(grams, roots, products, norms)]


def total(values):
    while len(values) > 1:
        values = [sum(values[i + 1 : i + 2], values[i]) for i in range(0, len(values), 2)]
    return values[0]


def vmem_call(kernel, outs, args, scratch=(), places={}):
    return pl.pallas_call(
        kernel,
        out_shape=[jax.ShapeDtypeStruct(shape, F32) for shape in outs],
        in_specs=[pl.BlockSpec(memory_space=places.get(i, pltpu.VMEM)) for i in range(len(args))],
        out_specs=[pl.BlockSpec(memory_space=pltpu.VMEM) for _ in outs],
        scratch_shapes=list(scratch),
        compiler_params=pltpu.CompilerParams(vmem_limit_bytes=VMEM_LIMIT),
    )(*args)


def add_gram(x, main_ref, edge_ref):
    high, mid, low = split(x)
    both = cat(high, mid)
    main_ref[...] += bdot(both, both, ROWS_BY_ROWS)
    edge_ref[...] += bdot(high, low, ROWS_BY_ROWS)


def gram_total(main_ref, edge_ref):
    n = edge_ref.shape[1]
    main, edge = main_ref[...], edge_ref[...]
    return main[:n, :n] + ((main[:n, n:] + main[n:, :n]) + (main[n:, n:] + (edge + edge.T)))


def gram_scratch(width):
    return [pltpu.VMEM((2 * width, 2 * width), F32), pltpu.VMEM((width, width), F32)]


def clear(*refs):
    for ref in refs:
        ref[...] = jnp.zeros_like(ref)


def each_chunk(rows, step):
    lax.fori_loop(0, rows // CHUNK, lambda i, _: step(pl.multiple_of(i * CHUNK, CHUNK)), None)


def scalars_kernel(bits, partner, place, first, middle, last, lead, closing, exchanges):
    strides = [partner[index, 0] for index in range(ROUNDS - 1)]
    zero = jnp.int32(0)
    which = [sum(((s >= 1 << bit).astype(jnp.int32) for bit in range(1, bits)), zero) for s in strides]
    first[0], middle[0], last[0] = which
    early, late = (which[0] == which[1]).astype(jnp.int32), (which[1] == which[2]).astype(jnp.int32)
    leap = jnp.where(which[0] < which[1], 1 - late, 0)
    place[0] = jnp.where(leap == 1, which[0], which[1])
    lead[0] = 1 - early - leap
    closing[0] = 1 - late + leap
    exchanges[...] = jnp.full(exchanges.shape, 1 + early + late, jnp.int32)


def pair_bits():
    return lax.axis_size("pair").bit_length() - 1


def scalars(partner):
    space = pl.BlockSpec(memory_space=pltpu.SMEM)
    return pl.pallas_call(
        functools.partial(scalars_kernel, pair_bits()),
        out_shape=[jax.ShapeDtypeStruct((1,), jnp.int32)] * 6 + [jax.ShapeDtypeStruct((8, 128), jnp.int32)],
        in_specs=[space],
        out_specs=[space] * 6 + [pl.BlockSpec(memory_space=pltpu.VMEM)],
    )(partner)


def upper_in(bit):
    return 0 if bit is None else jnp.bitwise_and(jnp.right_shift(lax.axis_index("pair"), bit), 1)


def halves_kernel(bit, x_hbm, kept_ref, rest_ref, sems):
    half, upper = kept_ref.shape[0], upper_in(bit)
    copies = [
        pltpu.make_async_copy(x_hbm.at[pl.ds(pl.multiple_of(at * half, half), half)], ref, sems.at[i])
        for i, (at, ref) in enumerate(((1 - upper, rest_ref), (upper, kept_ref)))
    ]
    for copy in copies:
        copy.start()
    for copy in copies:
        copy.wait()


def halves(bit, x):
    rows, width = x.shape
    outs = [(rows // 2, width)] * 2
    scratch = [pltpu.SemaphoreType.DMA((2,))]
    return vmem_call(functools.partial(halves_kernel, bit), outs, [x], scratch, {0: pl.ANY})


def gram_kernel(kept_ref, rest_ref, gram_ref, *scratch):
    clear(*scratch)
    for ref in (kept_ref, rest_ref):
        add_gram(ref[...], *scratch)
    gram_ref[...] = gram_total(*scratch)


def gram(kept, rest):
    width = kept.shape[1]
    return vmem_call(gram_kernel, [(width, width)], [kept, rest], gram_scratch(width))[0]


def in_order(upper, a, b):
    return (jnp.where(upper == 1, b, a), jnp.where(upper == 1, a, b)) if isinstance(upper, jax.Array) else (a, b)


def second_half(shape):
    return lax.broadcasted_iota(jnp.int32, shape, 1) >= shape[1] // 2


def merge_kernel(bit, x_ref, folded_ref, kept_ref, rest_ref, *refs):
    half, width = folded_ref.shape
    second, upper = second_half((CHUNK, width)), upper_in(bit)
    clear(*refs[1:])

    def step(at):
        rows = pl.ds(at, CHUNK)
        folded = folded_ref[rows, :]
        top = jnp.where(second, pltpu.roll(folded, width // 2, 1), x_ref[rows, :])
        bottom = jnp.where(second, folded, x_ref[pl.ds(half + at, CHUNK), :])
        kept_ref[rows, :], rest_ref[rows, :] = in_order(upper, top, bottom)
        if refs:
            add_gram(cat(top, bottom, axis=0), *refs[1:])

    each_chunk(half, step)
    if refs:
        refs[0][...] = gram_total(*refs[1:])


def merge(bit, x, folded, with_gram=True):
    width = x.shape[1]
    outs = [folded.shape] * 2 + [(width, width)] * with_gram
    scratch = gram_scratch(width) if with_gram else []
    return vmem_call(functools.partial(merge_kernel, bit), outs, [x, folded], scratch)


def write_rows(upper, sources, out_ref, folded_ref=None):
    half, width = sources[0][0].shape
    second = second_half((CHUNK, width))

    def step(at):
        rows = pl.ds(at, CHUNK)
        kept, rest = (
            total([dot_packed(pair[i][rows, :], packed) for *pair, packed in sources]) for i in range(2)
        )
        out_ref[pl.ds(pl.multiple_of(upper * half + at, CHUNK), CHUNK), :] = kept
        out_ref[pl.ds(pl.multiple_of((1 - upper) * half + at, CHUNK), CHUNK), :] = rest
        if folded_ref is None:
            return
        top, bottom = in_order(upper, kept, rest)
        folded_ref[rows, :] = jnp.where(second, bottom, pltpu.roll(top, width // 2, 1))

    each_chunk(half, step)


def rows_call(kernel, args, kept, fold=True):
    half, width = kept.shape
    return vmem_call(kernel, [(2 * half, width)] + [kept.shape] * fold, args)


def rotate_kernel(bit, count, kept_ref, rest_ref, *refs):
    gram_sum = total([part[...] for part in refs[:count]])
    rotation = pack_right(orthogonalizers([gram_sum])[0][0])
    write_rows(upper_in(bit), [(kept_ref, rest_ref, rotation)], *refs[count:])


def rotate(bit, kept, rest, parts, fold):
    kernel = functools.partial(rotate_kernel, bit, len(parts))
    return rows_call(kernel, [kept, rest, *parts], kept, fold)


def cross_kernel(bit, own_ref, other_ref, gram_ref, sent_ref):
    n = own_ref.shape[1]
    high, mid, low = split(own_ref[...])
    other_high, other_mid, other_low = split(other_ref[...])
    main = bdot(cat(high, mid), cat(other_high, other_mid), ROWS_BY_ROWS)
    edge = bdot(high, other_low, ROWS_BY_ROWS) + bdot(low, other_high, ROWS_BY_ROWS)
    cross = main[:n, :n] + ((main[:n, n:] + main[n:, :n]) + (main[n:, n:] + edge))
    sent_ref[:n, :] = jnp.where(upper_in(bit) == 1, cross.T, cross)
    sent_ref[n:, :] = gram_ref[...]


def cross_gram(bit, own, other, own_gram):
    width = own.shape[1]
    return vmem_call(functools.partial(cross_kernel, bit), [(2 * width, width)], [own, other, own_gram])[0]


def join_kernel(sent_ref, got_ref, own_ref, sum_ref, copy_ref):
    n = sum_ref.shape[0]
    sum_ref[...] = sent_ref[:n, :] + got_ref[:n, :]
    copy_ref[...] = own_ref[...]


def join(sent, got, own):
    return vmem_call(join_kernel, [(sent.shape[1],) * 2, own.shape], [sent, got, own])


def first_kernel(own_ref, other_ref, *outs):
    n = own_ref.shape[1]
    pair = orthogonalizers([own_ref[n:, :], other_ref[n:, :]], True)
    (outs[0][...], outs[1][...], outs[2][...]), (outs[3][...], _, outs[4][...]) = pair


def first_rotations(sent, got):
    return vmem_call(first_kernel, [(sent.shape[1],) * 2] * 5, [sent, got])


def run_kernel(count, bit, exchanges, v0, t0, g0, v1, g1, *refs):
    parts, (from_own, from_other) = refs[:count], refs[count:]
    n = v0.shape[0]
    row, col = indices(n)
    first_row, first_col = row < n // 2, col < n // 2

    def by_block(aa, ab, ba, bb):
        return jnp.where(first_row, jnp.where(first_col, aa, ab), jnp.where(first_col, ba, bb))

    def trade(own, other, cross, own_map, other_map):
        flipped = cross.T
        return (
            by_block(own, cross, flipped, other),
            by_block(other, flipped, cross, own),
            by_block(cross, own, other, flipped),
            [jnp.where(first_col, a, b) for a, b in zip(own_map, other_map)],
            [jnp.where(first_col, b, a) for a, b in zip(own_map, other_map)],
        )

    def step(_, state):
        own, other, cross, own_map, other_map = trade(*state)
        (v, t, own), (w, _, other) = orthogonalizers([own, other], True, 2)
        v, w = pack_right(v), pack_right(w)
        cross = dot(t, dot_packed(cross, w))
        return own, other, cross, [dot_packed(m, v) for m in own_map], [dot_packed(m, w) for m in other_map]

    cross = total([part[...] for part in parts])
    cross = jnp.where(upper_in(bit) == 1, cross.T, cross)
    cross = dot(t0[...], dot(cross, v1[...]))
    zeros = jnp.zeros((n, n), F32)
    state = g0[...], g1[...], cross, [v0[...], zeros], [zeros, v1[...]]
    from_own[...], from_other[...] = lax.fori_loop(0, jnp.max(exchanges[...]), step, state)[3]


def run_maps(bit, exchanges, first, parts):
    args = [exchanges, *first, *parts]
    outs = [parts[0].shape] * 2
    return vmem_call(functools.partial(run_kernel, len(parts), bit), outs, args)


def apply_kernel(bit, kept, rest, kept_other, rest_other, from_own, from_other, *outs):
    own, other = pack_right(from_own[...]), pack_right(from_other[...])
    write_rows(upper_in(bit), [(kept, rest, own), (kept_other, rest_other, other)], *outs)


def apply_maps(bit, kept, rest, kept_other, rest_other, maps):
    return rows_call(functools.partial(apply_kernel, bit), [kept, rest, kept_other, rest_other, *maps], kept)


def swap(value, axis, mask):
    return lax.ppermute(value, axis, [(i, i ^ mask) for i in range(lax.axis_size(axis))])


def row_sum_parts(value):
    masks = [1 << bit for bit in range(lax.axis_size("row").bit_length() - 1)]
    parts = [value, swap(value, "row", masks[0])]
    for start in range(1, len(masks), 2):
        value = total(parts)
        near = masks[start : start + 2]
        reach = ([near[0] ^ near[1]] if len(near) == 2 else []) + near
        parts = [value] + [swap(value, "row", mask) for mask in reach]
    return parts


def pair_swap(mask, value):
    return swap(value, "pair", mask)


def by_stride(bit, function, *args):
    return lax.switch(bit, [functools.partial(function, 1 << b) for b in range(pair_bits())], *args)


def run(bit, exchanges, kept, rest):
    mask = 1 << bit
    kept_other = swap(rest, "pair", mask)
    own_gram = total(row_sum_parts(gram(kept, rest)))
    sent = cross_gram(bit, kept, kept_other, own_gram)
    got = swap(sent, "pair", mask)
    cross, kept_again = join(sent, got, kept)
    rest_other = swap(kept_again, "pair", mask)
    first = first_rotations(sent, got)
    maps = run_maps(bit, exchanges, first, row_sum_parts(cross))
    return apply_maps(bit, kept, rest, kept_other, rest_other, maps)


def one_round(bit, kept, rest, local, fold=True):
    return rotate(bit, kept, rest, row_sum_parts(local), fold)


def rounds(bit, matrix, first, middle, last, lead, closing, exchanges):
    kept, rest = halves(bit, matrix)

    def go_ahead(kept, rest):
        columns, folded = one_round(bit, kept, rest, gram(kept, rest))
        return tuple(merge(bit, columns, by_stride(first[0], pair_swap, folded), False))

    def follow(which, fold, columns, folded):
        return one_round(None, *merge(None, columns, by_stride(which[0], pair_swap, folded)), fold)

    def close(columns, folded):
        if bit + 1 < pair_bits():
            more = functools.partial(follow, middle, True)
            columns, folded = lax.cond(
                closing[0] == 2, lambda *args: tuple(more(*args)), lambda *args: args, columns, folded
            )
        return follow(last, False, columns, folded)[0]

    state = lax.cond(lead[0] == 1, go_ahead, lambda *state: state, kept, rest)
    columns, folded = run(bit, exchanges, *state)
    return lax.cond(closing[0] == 0, lambda columns, _: columns, close, columns, folded)


def body(matrix, partner):
    place, *others = scalars(partner)
    branches = [functools.partial(rounds, bit) for bit in range(pair_bits())]
    return lax.switch(place[0], branches, matrix, *others)


def solution(mesh):
    return jax.shard_map(
        body, mesh=mesh, in_specs=(P("row", "pair"), P()), out_specs=P("row", "pair"), check_vma=False
    )
```
